32 devices in a mesh: parts: 2 (over y), coef: 4 (over z), poly: 2 (over x), limb: 2 (over core).
Axes of the slice: x: 2, y: 2, z: 4, core: 2. Of those that a mesh axis runs over, the one named last changes fastest.
Arguments:
- coefficients: float32 [96, 128, 4096], P(('parts', 'poly', 'limb'), None, 'coef'), parts along dimension 0, may hold values from -6 to 6
- batch_weights: float32 [32, 48], P('parts', ('poly', 'limb')), parts along dimension 0, may hold values from -0.875 to 0.875
- claimed: float32 [2, 32, 48], P(None, 'parts', ('poly', 'limb')), parts along dimension 1, may hold values from -6 to 6
- point_index: int32 [32], P(('parts', 'poly', 'limb')), parts along dimension 0, may hold values from 0 to 524287
- point_cycle: int32 [32], P(('parts', 'poly', 'limb')), parts along dimension 0, may hold values from 0 to 3
Outputs:
- evaluations: float32 [2, 128, 96, 32, 128], P(None, 'coef', ('parts', 'poly', 'limb')), parts along dimension 2
- quotient: float32 [2, 32, 128, 4096], P(None, ('parts', 'poly', 'limb'), None, 'coef'), parts along dimension 1
The draws below stay inside these ranges and needn't reach their ends.
There are 2 independent parts, one for each index of `parts`. The reference program is written for one: setup_inputs(seed, part) draws one part's arguments, and reference() takes and returns one part's arrays. A program takes and returns all parts, laid end to end along the dimension named above; each array names one. Nothing has to cross between parts.
All inputs are finite; a program needn't handle non-finite values.
Results may differ from the reference program's by a relative error of at most 0.0003.
Values sent between devices are 32-bit elements; how exact they have to be, the bound alone decides.
No kernel may reach another device: no remote copies, remote signals or barrier semaphores. Data moves between devices by JAX's collectives and lax.ppermute only.
A program may use at most 128 MiB of HBM per device.

```python
import math
import jax
import jax.numpy as jnp
from jax import lax

POLYS = 48
COLUMNS = 16
LEN_COLS = 128
SPLIT_HI = 32
SPLIT_LO = 128
LEN_ROWS = 4096
LENGTH = 524288


def with_ends(result, key, least, top_value):
    shape = result.shape
    place = [jax.random.randint(jax.random.fold_in(key, axis), (), 0, shape[axis]) for axis in range(len(shape))]
    result = result.at[tuple(place)].set(least)
    longest = shape.index(max(shape))
    place[longest] = (place[longest] + 1) % shape[longest]
    return result.at[tuple(place)].set(top_value)


def steps_of(rng, extent, split, smallest, largest):
    def one(axis_at, blocks):
        steps = jax.random.uniform(jax.random.fold_in(jax.random.fold_in(rng, 6), axis_at), (blocks,), jnp.float32, smallest / len(split), largest / len(split))
        return jnp.repeat(jnp.exp(steps), extent[axis_at] // blocks).reshape((-1,) + (1,) * (len(extent) - axis_at - 1))

    factor_of = one(*split[0])
    for cut in split[1:]:
        factor_of = factor_of * one(*cut)
    return factor_of


def centred(own_key, dims, scale, reach, pieces=(), held_as=jnp.bfloat16):
    entries = jax.random.normal(own_key, dims, jnp.float32) * scale
    if len(pieces) > 0:
        entries = steps_of(own_key, dims, pieces, -0.22, 0.18) * entries
    return jnp.clip(entries, min=-reach, max=reach).astype(held_as)


def setup_inputs(seed: int = 0, part: int = 0) -> dict:
    keys = jax.random.split(jax.random.key(seed), 6)
    part_keys = jax.random.split(jax.random.fold_in(keys[5], part), 6)
    return {
        "coefficients": centred(part_keys[0], (POLYS, LEN_COLS, LEN_ROWS), 1.0, 6.0, ((0, 4), (2, 4)), jnp.float32),
        "batch_weights": centred(part_keys[1], (COLUMNS, POLYS), POLYS ** -0.5, 0.875, ((1, 4),), jnp.float32),
        "claimed": centred(part_keys[2], (2, COLUMNS, POLYS), 1.0, 6.0, ((2, 4),), jnp.float32),
        "point_index": with_ends(jax.random.randint(part_keys[3], (COLUMNS,), 0, LENGTH), jax.random.fold_in(part_keys[3], 1), 0, LENGTH - 1).astype(jnp.int32),
        "point_cycle": with_ends(jax.random.randint(part_keys[4], (COLUMNS,), 0, 4), jax.random.fold_in(part_keys[4], 1), 0, 3).astype(jnp.int32),
    }


def arrange(values):
    return values.reshape(POLYS, SPLIT_LO, SPLIT_HI, LEN_COLS).transpose(3, 0, 2, 1)

def reference(coefficients, batch_weights, claimed, point_index, point_cycle):
    root_length = math.sqrt(LENGTH)
    flattened = coefficients.reshape(POLYS, LENGTH)
    spectrum = jnp.fft.fft(flattened, axis=1) / root_length
    spec_real = jnp.real(spectrum)
    spec_imag = jnp.imag(spectrum)
    evaluations = jnp.stack([arrange(spec_real), arrange(spec_imag)])
    offsets = lax.optimization_barrier(jnp.sum(batch_weights[None] * claimed, axis=2))
    numer_real = jnp.dot(batch_weights, spec_real, precision=lax.Precision.HIGHEST) - offsets[0][:, None]
    numer_imag = jnp.dot(batch_weights, spec_imag, precision=lax.Precision.HIGHEST) - offsets[1][:, None]
    positions = jnp.arange(LENGTH, dtype=jnp.int32)
    angles = positions.astype(jnp.float32) * (2.0 * math.pi / LENGTH)
    point_angle = point_index.astype(jnp.float32) * (2.0 * math.pi / LENGTH)
    radius = 1.0 + (point_cycle.astype(jnp.float32) + 1.0) / 512.0
    diff_real = jnp.cos(angles)[None, :] - (radius * jnp.cos(point_angle))[:, None]
    diff_imag = (radius * jnp.sin(point_angle))[:, None] - jnp.sin(angles)[None, :]
    magnitude = diff_real * diff_real + diff_imag * diff_imag
    quot_real = (numer_real * diff_real + numer_imag * diff_imag) / magnitude
    quot_imag = (numer_imag * diff_real - numer_real * diff_imag) / magnitude
    coeffs = jnp.fft.ifft(quot_real + 1j * quot_imag, axis=1) * root_length
    quotient = jnp.stack([jnp.real(coeffs), jnp.imag(coeffs)]).reshape(2, COLUMNS, LEN_COLS, LEN_ROWS)
    return (evaluations, quotient)
```

```python
import functools
import math

import jax
import jax.numpy as jnp
import ml_dtypes
import numpy as np
from jax import lax
from jax.experimental import pallas as pl
from jax.experimental.pallas import tpu as pltpu
from jax.sharding import PartitionSpec as P

LEN_COLS = 128
SPLIT_HI = 32
SPLIT_LO = 128
LEN_ROWS = 4096
LENGTH = 524288
VMEM_BYTES = 48 * 2**20

precise = lax.Precision.HIGHEST


def split(value):
    high = value.astype(jnp.bfloat16)
    low = (value - high.astype(jnp.float32)).astype(jnp.bfloat16)
    return high, low


def split_host(value):
    value = np.asarray(value, np.float32)
    high = value.astype(ml_dtypes.bfloat16)
    low = (value - high.astype(np.float32)).astype(ml_dtypes.bfloat16)
    return high, low


def roots(exponent, length):
    angles = np.asarray(exponent % length, np.float64) * (-2.0 * math.pi / length)
    return np.cos(angles), np.sin(angles)


def first_table(owners):
    index = np.arange(LEN_COLS, dtype=np.int64)
    pair = np.stack(roots(index[:, None] * index[None, :], LEN_COLS)) / math.sqrt(LEN_COLS)
    extent = LEN_COLS // owners
    table = pair.reshape(2, owners, extent, LEN_COLS).transpose(1, 0, 2, 3)
    table = table.reshape(2 * LEN_COLS, LEN_COLS)
    return np.concatenate([table, table]).astype(np.float32)


def middle_table(owners):
    frequency = np.arange(LEN_COLS, dtype=np.int64)
    extent = LEN_COLS // owners
    share = SPLIT_HI // owners
    sender = (frequency[:, None] // extent - np.arange(owners)[None, :]) % owners
    place = (sender[:, :, None] * share + np.arange(share)).reshape(LEN_COLS, 1, SPLIT_HI)
    slow = np.arange(SPLIT_HI, dtype=np.int64)[None, :, None]
    real, imag = roots(place * (LEN_COLS * slow + frequency[:, None, None]), LEN_ROWS)
    table = np.concatenate(
        [np.concatenate([real, -imag], axis=2), np.concatenate([imag, real], axis=2)], axis=1
    )
    high, low = split_host(table / math.sqrt(SPLIT_HI))
    return np.concatenate([high, low, high], axis=2)


def turn_table():
    frequency = np.arange(LEN_COLS, dtype=np.int64)[:, None, None]
    slow = np.arange(SPLIT_HI, dtype=np.int64)[None, :, None]
    fast = np.arange(SPLIT_LO, dtype=np.int64)[None, None, :]
    return np.stack(roots(fast * (frequency + LEN_COLS * slow), LENGTH), axis=1).astype(np.float32)


def last_table():
    index = np.arange(SPLIT_LO, dtype=np.int64)
    real, imag = roots(index[:, None] * index[None, :], SPLIT_LO)
    table = np.concatenate(
        [np.concatenate([real, imag], axis=1), np.concatenate([-imag, real], axis=1)], axis=0
    )
    high, low = split_host(table / math.sqrt(SPLIT_LO))
    return np.concatenate([high, high, low], axis=0)


def first_kernel(group, place_ref, table_ref, coeff_ref, *out_refs):
    owners = len(out_refs)
    rows = table_ref.shape[0] // 2
    each = rows // owners
    extent = each // 2
    begin = pl.multiple_of(place_ref[0] * each, each)
    high, low = split(table_ref[pl.ds(begin, rows), :])
    left = jnp.concatenate([high, low, high], axis=1)
    blocks = coeff_ref.shape[2] // SPLIT_LO
    step = min(2, blocks)
    for lane in range(0, blocks, step):
        value_high, value_low = split(coeff_ref[0, :, lane * SPLIT_LO:(lane + step) * SPLIT_LO])
        right = jnp.concatenate([value_high, value_high, value_low], axis=0)
        result = jnp.dot(left, right, preferred_element_type=jnp.float32)
        for inner in range(step):
            for owner in range(owners):
                for part in range(2):
                    for batch in range(extent // group):
                        top = owner * each + part * extent + batch * group
                        out_refs[owner][0, part, batch, pl.ds((lane + inner) * group, group), :] = result[
                            top:top + group, inner * SPLIT_LO:(inner + 1) * SPLIT_LO
                        ]


def first_section(place, table, coefficients, start, count, owners):
    rows_here = coefficients.shape[2]
    extent = LEN_COLS // owners
    group = min(8, extent)
    shape = (count, 2, extent // group, (rows_here // SPLIT_LO) * group, SPLIT_LO)
    return pl.pallas_call(
        functools.partial(first_kernel, group),
        out_shape=[jax.ShapeDtypeStruct(shape, jnp.float32)] * owners,
        grid_spec=pltpu.PrefetchScalarGridSpec(
            num_scalar_prefetch=1,
            grid=(count,),
            in_specs=[
                pl.BlockSpec(table.shape, lambda i, place: (0, 0)),
                pl.BlockSpec((1, LEN_COLS, rows_here), lambda i, place: (start + i, 0, 0)),
            ],
            out_specs=[pl.BlockSpec((1,) + shape[1:], lambda i, place: (i, 0, 0, 0, 0))] * owners,
        ),
        compiler_params=pltpu.CompilerParams(vmem_limit_bytes=VMEM_BYTES),
        cost_estimate=pl.CostEstimate(
            flops=count * 6 * 2 * LEN_COLS * LEN_COLS * rows_here,
            bytes_accessed=count * 12 * LEN_COLS * rows_here,
            transcendentals=0,
        ),
        name="first_section",
    )(place, table, coefficients)


def second_kernel(group, owners, aliased, place_ref, middle_ref, turn_ref, last_ref, *refs):
    piece_refs, out_ref = refs[:owners], refs[-1]
    count = out_ref.shape[2]
    share = SPLIT_HI // owners
    lines = []
    for item in range(group):
        columns = []
        for poly in range(count):
            pieces = []
            for part in range(2):
                for piece_ref in piece_refs:
                    if share == 1:
                        pieces.append(piece_ref[poly, part, 0, pl.ds(item, 1), :])
                    else:
                        pieces.append(piece_ref[poly, part, 0, pl.ds(item, share, stride=group), :])
            columns.append(jnp.concatenate(pieces, axis=0))
        gathered = columns[0] if count == 1 else jnp.concatenate(columns, axis=1)
        high, low = split(gathered)
        turned = jnp.dot(
            middle_ref[item], jnp.concatenate([high, high, low], axis=0), preferred_element_type=jnp.float32
        )
        cos_turn, sin_turn = turn_ref[item, 0], turn_ref[item, 1]
        for poly in range(count):
            lanes = slice(poly * SPLIT_LO, (poly + 1) * SPLIT_LO)
            real, imag = turned[:SPLIT_HI, lanes], turned[SPLIT_HI:, lanes]
            lines.append(
                jnp.concatenate([real * cos_turn - imag * sin_turn, real * sin_turn + imag * cos_turn], axis=1)
            )
    high, low = split(jnp.concatenate(lines, axis=0))
    result = jnp.dot(jnp.concatenate([high, low, high], axis=1), last_ref[...], preferred_element_type=jnp.float32)
    for item in range(group):
        for poly in range(count):
            top = (item * count + poly) * SPLIT_HI
            out_ref[0, item, poly] = result[top:top + SPLIT_HI, :SPLIT_LO]
            out_ref[1, item, poly] = result[top:top + SPLIT_HI, SPLIT_LO:]


def second_section(place, tables, pieces, previous, start, count, polys, owners):
    middle, turn, last = tables
    extent = LEN_COLS // owners
    group = min(8, extent)
    batches = extent // group
    block = (count, 2, 1) + pieces[0].shape[3:]
    in_specs = [
        pl.BlockSpec((group,) + middle.shape[1:], lambda i, place: (place[0] * batches + i, 0, 0)),
        pl.BlockSpec((group,) + turn.shape[1:], lambda i, place: (place[0] * batches + i, 0, 0, 0)),
        pl.BlockSpec(last.shape, lambda i, place: (0, 0)),
    ] + [pl.BlockSpec(block, lambda i, place: (0, 0, i, 0, 0))] * owners
    operands = [place, middle, turn, last] + list(pieces)
    aliases = {}
    if previous is not None:
        aliases = {len(operands): 0}
        operands.append(previous)
        in_specs.append(pl.BlockSpec(memory_space=pl.ANY))
    points = count * extent * LEN_ROWS
    return pl.pallas_call(
        functools.partial(second_kernel, group, owners, previous is not None),
        out_shape=jax.ShapeDtypeStruct((2, extent, polys, SPLIT_HI, SPLIT_LO), jnp.float32),
        grid_spec=pltpu.PrefetchScalarGridSpec(
            num_scalar_prefetch=1,
            grid=(batches,),
            in_specs=in_specs,
            out_specs=pl.BlockSpec(
                (2, group, count, SPLIT_HI, SPLIT_LO), lambda i, place: (0, i, start // count, 0, 0)
            ),
        ),
        input_output_aliases=aliases,
        compiler_params=pltpu.CompilerParams(vmem_limit_bytes=VMEM_BYTES),
        cost_estimate=pl.CostEstimate(
            flops=points * 6 * (4 * SPLIT_HI + 4 * SPLIT_LO), bytes_accessed=points * 24, transcendentals=0
        ),
        name="second_section",
    )(*operands)


def batch_kernel(weight_ref, coeff_ref, *out_refs):
    polys = coeff_ref.shape[0]
    columns = out_refs[0].shape[0]
    lanes = min(512, coeff_ref.shape[2])
    for top in range(0, coeff_ref.shape[1], 8):
        for lane in range(0, coeff_ref.shape[2], lanes):
            here = (slice(top, top + 8), slice(lane, lane + lanes))
            for target, out_ref in enumerate(out_refs):
                for column in range(columns):
                    row = target * columns + column
                    total = weight_ref[row, 0] * coeff_ref[(0,) + here]
                    for poly in range(1, polys):
                        total = total + weight_ref[row, poly] * coeff_ref[(poly,) + here]
                    out_ref[(column,) + here] = total


def batch_columns(weights, coefficients, targets):
    polys, extent, rows_here = coefficients.shape
    columns = weights.shape[0] // targets
    height = 16
    shape = (columns, extent, rows_here)
    return pl.pallas_call(
        batch_kernel,
        out_shape=[jax.ShapeDtypeStruct(shape, jnp.float32)] * targets,
        grid=(extent // height,),
        in_specs=[
            pl.BlockSpec(memory_space=pltpu.SMEM),
            pl.BlockSpec((polys, height, rows_here), lambda i: (0, i, 0)),
        ],
        out_specs=[pl.BlockSpec((columns, height, rows_here), lambda i: (0, i, 0))] * targets,
        compiler_params=pltpu.CompilerParams(vmem_limit_bytes=VMEM_BYTES),
        cost_estimate=pl.CostEstimate(
            flops=2 * weights.size * extent * rows_here,
            bytes_accessed=4 * (polys + weights.shape[0]) * extent * rows_here,
            transcendentals=0,
        ),
        name="batch_columns",
    )(weights, coefficients)


def filter_kernel(value_ref, table_ref, carry_ref, reach_ref, out_ref):
    table_high, table_low = split(table_ref[0])
    table = jnp.concatenate([table_high, table_high, table_low], axis=0)
    reach_real, reach_imag = reach_ref[0, 0:1, :], reach_ref[0, 1:2, :]
    blocks = value_ref.shape[2] // SPLIT_LO
    for block in range(blocks):
        lanes = slice(block * SPLIT_LO, (block + 1) * SPLIT_LO)
        high, low = split(value_ref[0, :, lanes])
        local = jnp.dot(jnp.concatenate([high, low, high], axis=1), table, preferred_element_type=jnp.float32)
        real = carry_ref[0, 0, :, block:block + 1]
        imag = carry_ref[1, 0, :, block:block + 1]
        out_ref[0, 0, :, lanes] = local[:, :SPLIT_LO] + (real * reach_real - imag * reach_imag)
        out_ref[1, 0, :, lanes] = local[:, SPLIT_LO:] + (real * reach_imag + imag * reach_real)


def filter_columns(values, table, carry, reach):
    columns, extent, rows_here = values.shape
    return pl.pallas_call(
        filter_kernel,
        out_shape=jax.ShapeDtypeStruct((2,) + values.shape, jnp.float32),
        grid=(columns,),
        in_specs=[
            pl.BlockSpec((1, extent, rows_here), lambda i: (i, 0, 0)),
            pl.BlockSpec((1,) + table.shape[1:], lambda i: (i, 0, 0)),
            pl.BlockSpec((2, 1) + carry.shape[2:], lambda i: (0, i, 0, 0)),
            pl.BlockSpec((1,) + reach.shape[1:], lambda i: (i, 0, 0)),
        ],
        out_specs=pl.BlockSpec((2, 1, extent, rows_here), lambda i: (0, i, 0, 0)),
        compiler_params=pltpu.CompilerParams(vmem_limit_bytes=VMEM_BYTES),
        cost_estimate=pl.CostEstimate(
            flops=6 * 2 * SPLIT_LO * values.size, bytes_accessed=12 * values.size, transcendentals=0
        ),
        name="filter_columns",
    )(values, table, carry, reach)


def times(left, right):
    return left[0] * right[0] - left[1] * right[1], left[0] * right[1] + left[1] * right[0]


def powers_of(point_index, point_cycle):
    decay = jnp.log1p((point_cycle.astype(jnp.float32) + 1.0) / 512.0)

    def powers(exponent):
        leading = (-1,) + (1,) * (exponent.ndim - 1)
        kept = jnp.exp(exponent.astype(jnp.float32) * -decay.reshape(leading))
        turns = (exponent * point_index.reshape(leading)) & (LENGTH - 1)
        angles = turns.astype(jnp.float32) * (2.0 * math.pi / LENGTH)
        return kept * jnp.cos(angles), kept * jnp.sin(angles)

    return powers


def masked(keep, pair):
    return jnp.where(keep, pair[0], 0.0), jnp.where(keep, pair[1], 0.0)


def quotient_columns(values, offsets, point_index, point_cycle):
    columns, extent, rows_here = values.shape
    blocks = rows_here // SPLIT_LO
    owners = LEN_ROWS // rows_here
    here = lax.axis_index("coef")
    powers = powers_of(point_index, point_cycle)

    offset = jnp.arange(rows_here, dtype=jnp.int32)[None, :, None]
    border = SPLIT_LO * (1 + jnp.arange(blocks, dtype=jnp.int32))[None, None, :]
    distance = border - 1 - offset
    weights = masked(distance >= 0, powers(jnp.maximum(distance, 0)))
    weights = jnp.concatenate(weights, axis=2)
    ends = jnp.einsum("jnm,jmq->jnq", values, weights, precision=precise)
    ends = ends.reshape(columns, extent, 2, blocks).transpose(2, 0, 1, 3)

    gathered = lax.all_gather(ends[:, :, :, blocks - 1], "coef", axis=0)
    owner = jnp.arange(owners, dtype=jnp.int32)
    weigh = powers(rows_here * (owners - 1 - owner)[None, :, None])
    segment = (gathered[:, 0].transpose(1, 0, 2), gathered[:, 1].transpose(1, 0, 2))
    row_end = times(weigh, segment)
    row_end = (jnp.sum(row_end[0], axis=1), jnp.sum(row_end[1], axis=1))
    radius = 1.0 + (point_cycle.astype(jnp.float32) + 1.0) / 512.0
    angle = point_index.astype(jnp.float32) * (2.0 * math.pi / LENGTH)
    point = (radius * jnp.cos(angle), -radius * jnp.sin(angle))
    shift = times(point, (offsets[0] * math.sqrt(LENGTH), offsets[1] * math.sqrt(LENGTH)))
    final = jnp.arange(extent, dtype=jnp.int32)[None, :] == extent - 1
    row_end = tuple(value - jnp.where(final, moved[:, None], 0.0) for value, moved in zip(row_end, shift))
    row = jnp.arange(extent, dtype=jnp.int32)
    since = (row[:, None] - row[None, :] - 1) % extent
    kernel = powers(LEN_ROWS * since[None])
    around = 1.0 / (1.0 - jnp.exp(-float(LENGTH) * jnp.log1p((point_cycle.astype(jnp.float32) + 1.0) / 512.0)))
    kernel = (kernel[0] * around[:, None, None], kernel[1] * around[:, None, None])

    def apply(matrix, vector):
        return jnp.sum(matrix * vector[:, None, :], axis=2)

    row_start = (
        apply(kernel[0], row_end[0]) - apply(kernel[1], row_end[1]),
        apply(kernel[0], row_end[1]) + apply(kernel[1], row_end[0]),
    )

    ahead = here - 1 - owner
    within = times(masked(ahead >= 0, powers(rows_here * jnp.maximum(ahead, 0)[None, :])), (1.0, 0.0))
    within = times((within[0][:, :, None], within[1][:, :, None]), segment)
    segment_start = times(powers((rows_here * here)[None, None]), row_start)
    segment_start = tuple(start + jnp.sum(part, axis=1) for start, part in zip(segment_start, within))
    block = SPLIT_LO * jnp.arange(blocks, dtype=jnp.int32)[None, None, :]
    carry = times(powers(block), (segment_start[0][:, :, None], segment_start[1][:, :, None]))
    carry = jnp.stack(carry) + jnp.pad(ends[:, :, :, : blocks - 1], ((0, 0), (0, 0), (0, 0), (1, 0)))

    lane = jnp.arange(SPLIT_LO, dtype=jnp.int32)
    apart = (lane[None, :] - lane[:, None])[None]
    inside = masked(apart >= 0, powers(jnp.maximum(apart, 0) + 1))
    table = -jnp.concatenate(inside, axis=2)
    reach = -jnp.stack(powers((lane + 2)[None, :]), axis=1)
    return filter_columns(values, table, carry, reach)


def chunk_sizes(polys):
    sizes = [1, 1]
    while sum(sizes) + 2 + 2 <= polys:
        sizes.append(2)
    while sum(sizes) < polys:
        sizes.append(1)
    return sizes


def exchange(pieces, owners):
    if owners <= 8:
        moved = [
            lax.ppermute(pieces[far], "coef", [(i, (i + far) % owners) for i in range(owners)])
            for far in range(1, owners)
        ]
        return [pieces[0]] + moved
    here = lax.axis_index("coef")
    stacked = jnp.stack(pieces)
    stacked = jnp.roll(stacked, here, axis=0)
    stacked = lax.all_to_all(stacked, "coef", split_axis=0, concat_axis=0, tiled=True)
    stacked = jnp.roll(stacked[::-1], here + 1, axis=0)
    return [stacked[far] for far in range(owners)]


def shift_sum(pieces, axis, size):
    total = pieces[0]
    for far in range(1, size):
        total = total + lax.ppermute(pieces[far], axis, [(i, (i + far) % size) for i in range(size)])
    return total


def shards(coefficients, batch_weights, claimed, point_index, point_cycle, sizes):
    owners, poly_size, limb_size = sizes
    polys = coefficients.shape[0]
    here = lax.axis_index("coef")
    place = here.astype(jnp.int32)[None]
    table = jnp.asarray(first_table(owners))
    tables = (jnp.asarray(middle_table(owners)), jnp.asarray(turn_table()), jnp.asarray(last_table()))

    chunks = []
    start = 0
    for count in chunk_sizes(polys):
        chunks.append((start, count))
        start += count

    arrived = []
    for number, (start, count) in enumerate(chunks):
        pieces = first_section(place, table, coefficients, start, count, owners)
        if number >= 2:
            pieces, arrived[number - 2] = lax.optimization_barrier((pieces, arrived[number - 2]))
        arrived.append(exchange(pieces, owners))

    targets = poly_size * limb_size
    columns = batch_weights.shape[0] // targets
    ahead = jnp.arange(poly_size, dtype=jnp.int32)[:, None] + lax.axis_index("poly")
    aside = jnp.arange(limb_size, dtype=jnp.int32)[None, :] + lax.axis_index("limb")
    target = ((ahead % poly_size) * limb_size + aside % limb_size).reshape(-1)
    ordered = batch_weights.reshape(targets, columns, polys)[target].reshape(batch_weights.shape)
    batched = batch_columns(ordered, coefficients, targets)
    by_poly = [
        shift_sum(batched[far * limb_size:(far + 1) * limb_size], "limb", limb_size) for far in range(poly_size)
    ]
    values = shift_sum(by_poly, "poly", poly_size)
    offsets = lax.psum(jnp.sum(batch_weights[None] * claimed, axis=2), ("poly", "limb"))
    me = lax.axis_index("poly") * limb_size + lax.axis_index("limb")
    offsets = lax.dynamic_slice_in_dim(offsets, me * columns, columns, axis=1)
    quotient = quotient_columns(values, offsets, point_index, point_cycle)

    evaluations = None
    for (start, count), pieces in zip(chunks, arrived):
        evaluations = second_section(place, tables, pieces, evaluations, start, count, polys, owners)
    return (evaluations, quotient)


def solution(mesh):
    placed = (
        P(("parts", "poly", "limb"), None, "coef"),
        P("parts", ("poly", "limb")),
        P(None, "parts", ("poly", "limb")),
        P(("parts", "poly", "limb")),
        P(("parts", "poly", "limb")),
    )
    sizes = tuple(mesh.shape[name] for name in ("coef", "poly", "limb"))
    return jax.shard_map(
        functools.partial(shards, sizes=sizes),
        mesh=mesh,
        in_specs=placed,
        out_specs=(
            P(None, "coef", ("parts", "poly", "limb"), None, None),
            P(None, ("parts", "poly", "limb"), None, "coef"),
        ),
        check_vma=False,
    )
```

```python
import functools
import math

import jax
import jax.numpy as jnp
import ml_dtypes
import numpy as np
from jax import lax
from jax.experimental import pallas as pl
from jax.experimental.pallas import tpu as pltpu
from jax.sharding import PartitionSpec as P

LEN_COLS = 128
SPLIT_HI = 32
SPLIT_LO = 128
LEN_ROWS = 4096
LENGTH = 524288
VMEM_BYTES = 48 * 2**20

SMALL_COST = pl.CostEstimate(flops=1, bytes_accessed=1, transcendentals=0)
DEPTH = 4

precise = lax.Precision.HIGHEST


def split(value):
    high = value.astype(jnp.bfloat16)
    low = (value - high.astype(jnp.float32)).astype(jnp.bfloat16)
    return high, low


def split_host(value):
    value = np.asarray(value, np.float32)
    high = value.astype(ml_dtypes.bfloat16)
    low = (value - high.astype(np.float32)).astype(ml_dtypes.bfloat16)
    return high, low


def roots(exponent, length):
    angles = np.asarray(exponent % length, np.float64) * (-2.0 * math.pi / length)
    return np.cos(angles), np.sin(angles)


def first_table(owners):
    index = np.arange(LEN_COLS, dtype=np.int64)
    pair = np.stack(roots(index[:, None] * index[None, :], LEN_COLS)) / math.sqrt(LEN_COLS)
    extent = LEN_COLS // owners
    table = pair.reshape(2, owners, extent, LEN_COLS).transpose(1, 0, 2, 3)
    table = table.reshape(2 * LEN_COLS, LEN_COLS)
    return np.concatenate([table, table]).astype(np.float32)


def middle_table(owners):
    frequency = np.arange(LEN_COLS, dtype=np.int64)
    extent = LEN_COLS // owners
    share = SPLIT_HI // owners
    sender = (frequency[:, None] // extent - np.arange(owners)[None, :]) % owners
    place = (sender[:, :, None] * share + np.arange(share)).reshape(LEN_COLS, 1, SPLIT_HI)
    slow = np.arange(SPLIT_HI, dtype=np.int64)[None, :, None]
    real, imag = roots(place * (LEN_COLS * slow + frequency[:, None, None]), LEN_ROWS)
    table = np.concatenate(
        [np.concatenate([real, -imag], axis=2), np.concatenate([imag, real], axis=2)], axis=1
    )
    high, low = split_host(table / math.sqrt(SPLIT_HI))
    return np.concatenate([high, low, high], axis=2)


def turn_table():
    frequency = np.arange(LEN_COLS, dtype=np.int64)[:, None, None]
    slow = np.arange(SPLIT_HI, dtype=np.int64)[None, :, None]
    fast = np.arange(SPLIT_LO, dtype=np.int64)[None, None, :]
    return np.stack(roots(fast * (frequency + LEN_COLS * slow), LENGTH), axis=1).astype(np.float32)


def last_table():
    index = np.arange(SPLIT_LO, dtype=np.int64)
    real, imag = roots(index[:, None] * index[None, :], SPLIT_LO)
    table = np.concatenate(
        [np.concatenate([real, imag], axis=1), np.concatenate([-imag, real], axis=1)], axis=0
    )
    high, low = split_host(table / math.sqrt(SPLIT_LO))
    return np.concatenate([high, high, low], axis=0)


def transform(group, table_ref, coeff_ref, out_refs):
    owners = len(out_refs)
    rows = table_ref.shape[0] // 2
    each = rows // owners
    extent = each // 2
    begin = pl.multiple_of(lax.axis_index("coef") * each, each)
    high, low = split(table_ref[pl.ds(begin, rows), :])
    left = jnp.concatenate([high, low, high], axis=1)
    blocks = coeff_ref.shape[2] // SPLIT_LO
    step = min(2, blocks)
    for lane in range(0, blocks, step):
        value_high, value_low = split(coeff_ref[0, :, lane * SPLIT_LO:(lane + step) * SPLIT_LO])
        right = jnp.concatenate([value_high, value_high, value_low], axis=0)
        result = jnp.dot(left, right, preferred_element_type=jnp.float32)
        for inner in range(step):
            for owner in range(owners):
                for part in range(2):
                    for batch in range(extent // group):
                        top = owner * each + part * extent + batch * group
                        out_refs[owner][0, part, batch, pl.ds((lane + inner) * group, group), :] = result[
                            top:top + group, inner * SPLIT_LO:(inner + 1) * SPLIT_LO
                        ]


def batch(weight_ref, coeff_ref, out_refs):
    polys = coeff_ref.shape[0]
    lanes = min(512, coeff_ref.shape[2])
    for top in range(0, coeff_ref.shape[1], 8):
        for lane in range(0, coeff_ref.shape[2], lanes):
            here = (slice(top, top + 8), slice(lane, lane + lanes))
            for target, out_ref in enumerate(out_refs):
                for column in range(out_ref.shape[0]):
                    row = target * out_ref.shape[0] + column
                    total = weight_ref[row, 0] * coeff_ref[(0,) + here]
                    for poly in range(1, polys):
                        total = total + weight_ref[row, poly] * coeff_ref[(poly,) + here]
                    out_ref[(column,) + here] = total


def first_kernel(group, table_ref, coeff_ref, *out_refs):
    transform(group, table_ref, coeff_ref, out_refs)


def first_batch_kernel(group, count, owners, table_ref, coeff_ref, weight_ref, rows_ref, *out_refs):
    batch(weight_ref, rows_ref, out_refs[owners:])

    @pl.when(pl.program_id(0) < count)
    def _():
        transform(group, table_ref, coeff_ref, out_refs[:owners])


def first_section(table, coefficients, start, count, owners, weights=None, targets=1):
    polys, _, rows_here = coefficients.shape
    extent = LEN_COLS // owners
    group = min(8, extent)
    shape = (1, 2, extent // group, (rows_here // SPLIT_LO) * group, SPLIT_LO)
    steps = count
    kernel = functools.partial(first_kernel, group)
    in_specs = [
        pl.BlockSpec(table.shape, lambda i: (0, 0)),
        pl.BlockSpec((1, LEN_COLS, rows_here), lambda i: (start + jnp.minimum(i, count - 1), 0, 0)),
    ]
    out_specs = [pl.BlockSpec(shape, lambda i: (jnp.minimum(i, count - 1), 0, 0, 0, 0))] * owners
    out_shape = [jax.ShapeDtypeStruct((count,) + shape[1:], jnp.float32)] * owners
    operands = [table, coefficients]
    if weights is not None:
        columns = weights.shape[0] // targets
        height = 16 if count <= LEN_COLS // 16 else 8
        steps = LEN_COLS // height
        kernel = functools.partial(first_batch_kernel, group, count, owners)
        in_specs += [
            pl.BlockSpec(memory_space=pltpu.SMEM),
            pl.BlockSpec((polys, height, rows_here), lambda i: (0, i, 0)),
        ]
        out_specs += [pl.BlockSpec((columns, height, rows_here), lambda i: (0, i, 0))] * targets
        out_shape += [jax.ShapeDtypeStruct((columns, LEN_COLS, rows_here), jnp.float32)] * targets
        operands += [weights, coefficients]
    return list(
        pl.pallas_call(
            kernel,
            out_shape=out_shape,
            grid=(steps,),
            in_specs=in_specs,
            out_specs=out_specs,
            compiler_params=pltpu.CompilerParams(vmem_limit_bytes=VMEM_BYTES),
            cost_estimate=SMALL_COST,
            name="first_section",
        )(*operands)
    )


def second_kernel(group, owners, middle_ref, turn_ref, last_ref, *refs):
    piece_refs, out_ref = refs[:owners], refs[-1]
    count = out_ref.shape[2]
    share = SPLIT_HI // owners
    lines = []
    for item in range(group):
        places = pl.ds(item, 1) if share == 1 else pl.ds(item, share, stride=group)
        gathered = [
            jnp.concatenate(
                [piece_ref[poly, part, 0, places, :] for part in range(2) for piece_ref in piece_refs], axis=0
            )
            for poly in range(count)
        ]
        high, low = split(gathered[0] if count == 1 else jnp.concatenate(gathered, axis=1))
        turned = jnp.dot(
            middle_ref[item], jnp.concatenate([high, high, low], axis=0), preferred_element_type=jnp.float32
        )
        cos_turn, sin_turn = turn_ref[item, 0], turn_ref[item, 1]
        for poly in range(count):
            lanes = slice(poly * SPLIT_LO, (poly + 1) * SPLIT_LO)
            real, imag = turned[:SPLIT_HI, lanes], turned[SPLIT_HI:, lanes]
            lines.append(
                jnp.concatenate([real * cos_turn - imag * sin_turn, real * sin_turn + imag * cos_turn], axis=1)
            )
    high, low = split(jnp.concatenate(lines, axis=0))
    result = jnp.dot(jnp.concatenate([high, low, high], axis=1), last_ref[...], preferred_element_type=jnp.float32)
    for item in range(group):
        for poly in range(count):
            top = (item * count + poly) * SPLIT_HI
            out_ref[0, item, poly] = result[top:top + SPLIT_HI, :SPLIT_LO]
            out_ref[1, item, poly] = result[top:top + SPLIT_HI, SPLIT_LO:]


def second_section(tables, pieces, previous, start, count, polys, owners):
    middle, turn, last = tables
    extent = LEN_COLS // owners
    group = min(8, extent)
    together = 2 if start % 2 == 0 and count % 2 == 0 else 1
    first = start // together
    block = (together, 2, 1) + pieces[0].shape[3:]
    in_specs = [
        pl.BlockSpec((group,) + middle.shape[1:], lambda i, j: (i, 0, 0)),
        pl.BlockSpec((group,) + turn.shape[1:], lambda i, j: (i, 0, 0, 0)),
        pl.BlockSpec(last.shape, lambda i, j: (0, 0)),
    ] + [pl.BlockSpec(block, lambda i, j: (j, 0, i, 0, 0))] * owners
    operands = [middle, turn, last] + list(pieces)
    aliases = {}
    if previous is not None:
        aliases = {len(operands): 0}
        operands.append(previous)
        in_specs.append(pl.BlockSpec(memory_space=pl.ANY))
    return pl.pallas_call(
        functools.partial(second_kernel, group, owners),
        out_shape=jax.ShapeDtypeStruct((2, extent, polys, SPLIT_HI, SPLIT_LO), jnp.float32),
        grid=(extent // group, count // together),
        in_specs=in_specs,
        out_specs=pl.BlockSpec((2, group, together, SPLIT_HI, SPLIT_LO), lambda i, j: (0, i, first + j, 0, 0)),
        input_output_aliases=aliases,
        compiler_params=pltpu.CompilerParams(vmem_limit_bytes=VMEM_BYTES),
        cost_estimate=SMALL_COST,
        name="second_section",
    )(*operands)


def filter_kernel(value_ref, table_ref, carry_ref, reach_ref, out_ref):
    table_high, table_low = split(table_ref[0])
    table = jnp.concatenate([table_high, table_high, table_low], axis=0)
    reach_real, reach_imag = reach_ref[0, 0:1, :], reach_ref[0, 1:2, :]
    blocks = value_ref.shape[2] // SPLIT_LO
    for block in range(blocks):
        lanes = slice(block * SPLIT_LO, (block + 1) * SPLIT_LO)
        high, low = split(value_ref[0, :, lanes])
        local = jnp.dot(jnp.concatenate([high, low, high], axis=1), table, preferred_element_type=jnp.float32)
        real = carry_ref[0, 0, :, block:block + 1]
        imag = carry_ref[1, 0, :, block:block + 1]
        out_ref[0, 0, :, lanes] = local[:, :SPLIT_LO] + (real * reach_real - imag * reach_imag)
        out_ref[1, 0, :, lanes] = local[:, SPLIT_LO:] + (real * reach_imag + imag * reach_real)


def filter_columns(values, table, carry, reach):
    columns, extent, rows_here = values.shape
    return pl.pallas_call(
        filter_kernel,
        out_shape=jax.ShapeDtypeStruct((2,) + values.shape, jnp.float32),
        grid=(columns,),
        in_specs=[
            pl.BlockSpec((1, extent, rows_here), lambda i: (i, 0, 0)),
            pl.BlockSpec((1,) + table.shape[1:], lambda i: (i, 0, 0)),
            pl.BlockSpec((2, 1) + carry.shape[2:], lambda i: (0, i, 0, 0)),
            pl.BlockSpec((1,) + reach.shape[1:], lambda i: (i, 0, 0)),
        ],
        out_specs=pl.BlockSpec((2, 1, extent, rows_here), lambda i: (0, i, 0, 0)),
        compiler_params=pltpu.CompilerParams(vmem_limit_bytes=VMEM_BYTES),
        cost_estimate=SMALL_COST,
        name="filter_columns",
    )(values, table, carry, reach)


def times(left, right):
    return left[0] * right[0] - left[1] * right[1], left[0] * right[1] + left[1] * right[0]


def powers_of(point_index, point_cycle):
    decay = jnp.log1p((point_cycle.astype(jnp.float32) + 1.0) / 512.0)

    def powers(exponent):
        leading = (-1,) + (1,) * (exponent.ndim - 1)
        kept = jnp.exp(exponent.astype(jnp.float32) * -decay.reshape(leading))
        turns = (exponent * point_index.reshape(leading)) & (LENGTH - 1)
        angles = turns.astype(jnp.float32) * (2.0 * math.pi / LENGTH)
        return kept * jnp.cos(angles), kept * jnp.sin(angles)

    return powers


def masked(keep, pair):
    return jnp.where(keep, pair[0], 0.0), jnp.where(keep, pair[1], 0.0)


def segment_states(values, point_index, point_cycle):
    columns, extent, rows_here = values.shape
    blocks = rows_here // SPLIT_LO
    powers = powers_of(point_index, point_cycle)
    offset = jnp.arange(rows_here, dtype=jnp.int32)[None, :, None]
    border = SPLIT_LO * (1 + jnp.arange(blocks, dtype=jnp.int32))[None, None, :]
    distance = border - 1 - offset
    weights = masked(distance >= 0, powers(jnp.maximum(distance, 0)))
    weights = jnp.concatenate(weights, axis=2)
    ends = jnp.einsum("jnm,jmq->jnq", values, weights, precision=precise)
    return ends.reshape(columns, extent, 2, blocks).transpose(2, 0, 1, 3)


def from_all_owners(ends):
    owners = LEN_ROWS // (ends.shape[3] * SPLIT_LO)
    last = ends[:, :, :, -1]
    if owners <= 8:
        moved = [lax.ppermute(last, "coef", [(i, (i + far) % owners) for i in range(owners)]) for far in range(1, owners)]
        return jnp.stack([last] + moved)
    gathered = lax.all_gather(last, "coef", axis=0)
    return gathered[(lax.axis_index("coef") - jnp.arange(owners)) % owners]


def quotient_columns(values, ends, gathered, offsets, point_index, point_cycle):
    columns, extent, rows_here = values.shape
    blocks = rows_here // SPLIT_LO
    owners = LEN_ROWS // rows_here
    here = lax.axis_index("coef")
    powers = powers_of(point_index, point_cycle)

    owner = (here - jnp.arange(owners, dtype=jnp.int32)) % owners
    weigh = powers(rows_here * (owners - 1 - owner)[None, :, None])
    segment = (gathered[:, 0].transpose(1, 0, 2), gathered[:, 1].transpose(1, 0, 2))
    row_end = times(weigh, segment)
    row_end = (jnp.sum(row_end[0], axis=1), jnp.sum(row_end[1], axis=1))
    radius = 1.0 + (point_cycle.astype(jnp.float32) + 1.0) / 512.0
    angle = point_index.astype(jnp.float32) * (2.0 * math.pi / LENGTH)
    point = (radius * jnp.cos(angle), -radius * jnp.sin(angle))
    shift = times(point, (offsets[0] * math.sqrt(LENGTH), offsets[1] * math.sqrt(LENGTH)))
    final = jnp.arange(extent, dtype=jnp.int32)[None, :] == extent - 1
    row_end = tuple(value - jnp.where(final, moved[:, None], 0.0) for value, moved in zip(row_end, shift))
    row = jnp.arange(extent, dtype=jnp.int32)
    since = (row[:, None] - row[None, :] - 1) % extent
    kernel = powers(LEN_ROWS * since[None])
    around = 1.0 / (1.0 - jnp.exp(-float(LENGTH) * jnp.log1p((point_cycle.astype(jnp.float32) + 1.0) / 512.0)))
    kernel = (kernel[0] * around[:, None, None], kernel[1] * around[:, None, None])

    def apply(matrix, vector):
        return jnp.sum(matrix * vector[:, None, :], axis=2)

    row_start = (
        apply(kernel[0], row_end[0]) - apply(kernel[1], row_end[1]),
        apply(kernel[0], row_end[1]) + apply(kernel[1], row_end[0]),
    )

    ahead = here - 1 - owner
    within = times(masked(ahead >= 0, powers(rows_here * jnp.maximum(ahead, 0)[None, :])), (1.0, 0.0))
    within = times((within[0][:, :, None], within[1][:, :, None]), segment)
    segment_start = times(powers((rows_here * here)[None, None]), row_start)
    segment_start = tuple(start + jnp.sum(part, axis=1) for start, part in zip(segment_start, within))
    block = SPLIT_LO * jnp.arange(blocks, dtype=jnp.int32)[None, None, :]
    carry = times(powers(block), (segment_start[0][:, :, None], segment_start[1][:, :, None]))
    carry = jnp.stack(carry) + jnp.pad(ends[:, :, :, : blocks - 1], ((0, 0), (0, 0), (0, 0), (1, 0)))

    lane = jnp.arange(SPLIT_LO, dtype=jnp.int32)
    apart = (lane[None, :] - lane[:, None])[None]
    inside = masked(apart >= 0, powers(jnp.maximum(apart, 0) + 1))
    table = -jnp.concatenate(inside, axis=2)
    reach = -jnp.stack(powers((lane + 2)[None, :]), axis=1)
    return filter_columns(values, table, carry, reach)


def chunk_sizes(polys):
    most = (polys - 4) // 2
    return [1, most, polys - 4 - most, 2, 1] if polys > 6 else [1, 1, 2, 1, 1]


def exchange(pieces, owners, sent):
    if owners <= 8:
        moved = [pieces[0]]
        for far in range(1, owners):
            piece = pieces[far]
            if len(sent) >= DEPTH:
                chunk, place = sent[-DEPTH]
                piece, chunk[place] = lax.optimization_barrier((piece, chunk[place]))
            moved.append(lax.ppermute(piece, "coef", [(i, (i + far) % owners) for i in range(owners)]))
            sent.append((moved, far))
        return moved
    here = lax.axis_index("coef")
    stacked = jnp.roll(jnp.stack(pieces), here, axis=0)
    stacked = lax.all_to_all(stacked, "coef", split_axis=0, concat_axis=0, tiled=True)
    stacked = jnp.roll(stacked[::-1], here + 1, axis=0)
    return [stacked[far] for far in range(owners)]


def shift_sum(pieces, axis):
    size = len(pieces)
    total = pieces[0]
    for far in range(1, size):
        total = total + lax.ppermute(pieces[far], axis, [(i, (i + far) % size) for i in range(size)])
    return total


def shards(coefficients, batch_weights, claimed, point_index, point_cycle, sizes):
    owners, poly_size, limb_size = sizes
    polys = coefficients.shape[0]
    extent = LEN_COLS // owners
    table = jnp.asarray(first_table(owners))
    begin = lax.axis_index("coef") * extent
    tables = (
        lax.dynamic_slice_in_dim(jnp.asarray(middle_table(owners)), begin, extent, axis=0),
        lax.dynamic_slice_in_dim(jnp.asarray(turn_table()), begin, extent, axis=0),
        jnp.asarray(last_table()),
    )

    chunks = []
    start = 0
    for count in chunk_sizes(polys):
        chunks.append((start, count))
        start += count

    columns = batch_weights.shape[0] // (poly_size * limb_size)
    me_poly, me_limb = lax.axis_index("poly"), lax.axis_index("limb")
    ahead = (me_poly + jnp.arange(poly_size, dtype=jnp.int32)[None, :]) % poly_size
    aside = (me_limb + jnp.arange(limb_size, dtype=jnp.int32)[:, None]) % limb_size
    target = (ahead * limb_size + aside).reshape(-1)
    weights = batch_weights.reshape(-1, columns, polys)[target].reshape(batch_weights.shape)

    arrived = []
    sent = []
    used = 0
    evaluations = None
    for number, (start, count) in enumerate(chunks):
        batched = (weights, limb_size) if number == 1 else ()
        pieces = first_section(table, coefficients, start, count, owners, *batched)
        if number == 3:
            values = shift_sum([sums[i * columns:(i + 1) * columns] for i in range(poly_size)], "poly")
            ends = segment_states(values, point_index, point_cycle)
            pieces, ends = lax.optimization_barrier((pieces, ends))
        if number == len(chunks) - 1:
            while used < number - 2:
                evaluations = second_section(tables, arrived[used], evaluations, *chunks[used], polys, owners)
                used += 1
            gathered = from_all_owners(ends)
            quotient = quotient_columns(values, ends, gathered, offsets, point_index, point_cycle)
            pieces, quotient, evaluations = lax.optimization_barrier((pieces, quotient, evaluations))
        arrived.append(exchange(pieces[:owners], owners, sent))
        if number == 1:
            offsets = jnp.sum(batch_weights[None] * claimed, axis=2)
            pieces[owners:], arrived[0][1:], offsets = lax.optimization_barrier(
                (pieces[owners:], arrived[0][1:], offsets)
            )
            sums = shift_sum(pieces[owners:], "limb")
            offsets = lax.psum(offsets, ("poly", "limb"))
            offsets = lax.dynamic_slice_in_dim(offsets, (me_poly * limb_size + me_limb) * columns, columns, axis=1)

    for number in range(used, len(chunks)):
        evaluations = second_section(tables, arrived[number], evaluations, *chunks[number], polys, owners)
    return (evaluations, quotient)


def solution(mesh):
    placed = (
        P(("parts", "poly", "limb"), None, "coef"),
        P("parts", ("poly", "limb")),
        P(None, "parts", ("poly", "limb")),
        P(("parts", "poly", "limb")),
        P(("parts", "poly", "limb")),
    )
    return jax.shard_map(
        functools.partial(shards, sizes=tuple(mesh.shape[name] for name in ("coef", "poly", "limb"))),
        mesh=mesh,
        in_specs=placed,
        out_specs=(
            P(None, "coef", ("parts", "poly", "limb"), None, None),
            P(None, ("parts", "poly", "limb"), None, "coef"),
        ),
        check_vma=False,
    )
```

```python
import functools
import math

import jax
import jax.numpy as jnp
import ml_dtypes
import numpy as np
from jax import lax
from jax.experimental import pallas as pl
from jax.experimental.pallas import tpu as pltpu
from jax.sharding import PartitionSpec as P

LEN_COLS = 128
SPLIT_HI = 32
SPLIT_LO = 128
LEN_ROWS = 4096
LENGTH = 524288
VMEM_BYTES = 48 * 2**20

SMALL_COST = pl.CostEstimate(flops=1, bytes_accessed=1, transcendentals=0)
DEPTH = 5

precise = lax.Precision.HIGHEST


def split(value):
    high = value.astype(jnp.bfloat16)
    low = (value - high.astype(jnp.float32)).astype(jnp.bfloat16)
    return high, low


def split_host(value):
    value = np.asarray(value, np.float32)
    high = value.astype(ml_dtypes.bfloat16)
    low = (value - high.astype(np.float32)).astype(ml_dtypes.bfloat16)
    return high, low


def roots(exponent, length):
    angles = np.asarray(exponent % length, np.float64) * (-2.0 * math.pi / length)
    return np.cos(angles), np.sin(angles)


def first_table(owners):
    index = np.arange(LEN_COLS, dtype=np.int64)
    pair = np.stack(roots(index[:, None] * index[None, :], LEN_COLS)) / math.sqrt(LEN_COLS)
    extent = LEN_COLS // owners
    table = pair.reshape(2, owners, extent, LEN_COLS).transpose(1, 0, 2, 3)
    table = table.reshape(2 * LEN_COLS, LEN_COLS)
    return np.concatenate([table, table]).astype(np.float32)


def middle_table(owners):
    frequency = np.arange(LEN_COLS, dtype=np.int64)
    extent = LEN_COLS // owners
    share = SPLIT_HI // owners
    sender = (frequency[:, None] // extent - np.arange(owners)[None, :]) % owners
    place = (sender[:, :, None] * share + np.arange(share)).reshape(LEN_COLS, 1, SPLIT_HI)
    slow = np.arange(SPLIT_HI, dtype=np.int64)[None, :, None]
    real, imag = roots(place * (LEN_COLS * slow + frequency[:, None, None]), LEN_ROWS)
    table = np.concatenate(
        [np.concatenate([real, -imag], axis=2), np.concatenate([imag, real], axis=2)], axis=1
    )
    high, low = split_host(table / math.sqrt(SPLIT_HI))
    return np.concatenate([high, low, high], axis=2)


def turn_table():
    frequency = np.arange(LEN_COLS, dtype=np.int64)[:, None, None]
    slow = np.arange(SPLIT_HI, dtype=np.int64)[None, :, None]
    fast = np.arange(SPLIT_LO, dtype=np.int64)[None, None, :]
    return np.stack(roots(fast * (frequency + LEN_COLS * slow), LENGTH), axis=1).astype(np.float32)


def last_table():
    index = np.arange(SPLIT_LO, dtype=np.int64)
    real, imag = roots(index[:, None] * index[None, :], SPLIT_LO)
    table = np.concatenate(
        [np.concatenate([real, imag], axis=1), np.concatenate([-imag, real], axis=1)], axis=0
    )
    high, low = split_host(table / math.sqrt(SPLIT_LO))
    return np.concatenate([high, high, low], axis=0)


def transform(group, table_ref, coeff_ref, out_refs):
    owners = len(out_refs)
    rows = table_ref.shape[0] // 2
    each = rows // owners
    extent = each // 2
    begin = pl.multiple_of(lax.axis_index("coef") * each, each)
    high, low = split(table_ref[pl.ds(begin, rows), :])
    left = jnp.concatenate([high, low, high], axis=1)
    blocks = coeff_ref.shape[2] // SPLIT_LO
    step = min(2, blocks)
    for lane in range(0, blocks, step):
        value_high, value_low = split(coeff_ref[0, :, lane * SPLIT_LO:(lane + step) * SPLIT_LO])
        right = jnp.concatenate([value_high, value_high, value_low], axis=0)
        result = jnp.dot(left, right, preferred_element_type=jnp.float32)
        for inner in range(step):
            for owner in range(owners):
                for part in range(2):
                    for batch in range(extent // group):
                        top = owner * each + part * extent + batch * group
                        out_refs[owner][0, part, batch, pl.ds((lane + inner) * group, group), :] = result[
                            top:top + group, inner * SPLIT_LO:(inner + 1) * SPLIT_LO
                        ]


def batch(weight_ref, coeff_ref, out_refs):
    polys = coeff_ref.shape[0]
    lanes = min(512, coeff_ref.shape[2])
    for top in range(0, coeff_ref.shape[1], 8):
        for lane in range(0, coeff_ref.shape[2], lanes):
            here = (slice(top, top + 8), slice(lane, lane + lanes))
            for target, out_ref in enumerate(out_refs):
                for column in range(out_ref.shape[0]):
                    row = target * out_ref.shape[0] + column
                    total = weight_ref[row, 0] * coeff_ref[(0,) + here]
                    for poly in range(1, polys):
                        total = total + weight_ref[row, poly] * coeff_ref[(poly,) + here]
                    out_ref[(column,) + here] = total


def first_kernel(group, table_ref, coeff_ref, *out_refs):
    transform(group, table_ref, coeff_ref, out_refs)


def rest_kernel(group, counts, owners, table_ref, coeff_ref, weight_ref, rows_ref, *out_refs):
    step = pl.program_id(0)
    batch(weight_ref, rows_ref, out_refs[owners * len(counts):])
    begin = 0
    for number, count in enumerate(counts):

        @pl.when((step >= begin) & (step < begin + count))
        def _(number=number):
            transform(group, table_ref, coeff_ref, out_refs[number * owners:(number + 1) * owners])

        begin += count


def piece_shape(coefficients, count, owners):
    extent = LEN_COLS // owners
    group = min(8, extent)
    return (count, 2, extent // group, (coefficients.shape[2] // SPLIT_LO) * group, SPLIT_LO)


def first_section(table, coefficients, count, owners):
    rows_here = coefficients.shape[2]
    shape = piece_shape(coefficients, count, owners)
    pieces = pl.pallas_call(
        functools.partial(first_kernel, min(8, LEN_COLS // owners)),
        out_shape=[jax.ShapeDtypeStruct(shape, jnp.float32)] * owners,
        grid=(count,),
        in_specs=[
            pl.BlockSpec(table.shape, lambda i: (0, 0)),
            pl.BlockSpec((1, LEN_COLS, rows_here), lambda i: (i, 0, 0)),
        ],
        out_specs=[pl.BlockSpec((1,) + shape[1:], lambda i: (i, 0, 0, 0, 0))] * owners,
        compiler_params=pltpu.CompilerParams(vmem_limit_bytes=VMEM_BYTES),
        cost_estimate=SMALL_COST,
        name="first_section",
    )(table, coefficients)
    return list(pieces)


def rest_sections(table, coefficients, start, counts, owners, weights, targets):
    polys, _, rows_here = coefficients.shape
    columns = weights.shape[0] // targets
    total = sum(counts)
    height = 8
    steps = LEN_COLS // height
    out_specs, out_shape = [], []
    begin = 0
    for count in counts:
        shape = piece_shape(coefficients, count, owners)
        place = lambda i, begin=begin, count=count: (jnp.clip(i - begin, 0, count - 1), 0, 0, 0, 0)
        out_specs += [pl.BlockSpec((1,) + shape[1:], place)] * owners
        out_shape += [jax.ShapeDtypeStruct(shape, jnp.float32)] * owners
        begin += count
    out_specs += [pl.BlockSpec((columns, height, rows_here), lambda i: (0, jnp.minimum(i, steps - 1), 0))] * targets
    out_shape += [jax.ShapeDtypeStruct((columns, LEN_COLS, rows_here), jnp.float32)] * targets
    outs = pl.pallas_call(
        functools.partial(rest_kernel, min(8, LEN_COLS // owners), tuple(counts), owners),
        out_shape=out_shape,
        grid=(max(steps, total),),
        in_specs=[
            pl.BlockSpec(table.shape, lambda i: (0, 0)),
            pl.BlockSpec((1, LEN_COLS, rows_here), lambda i: (start + jnp.minimum(i, total - 1), 0, 0)),
            pl.BlockSpec(memory_space=pltpu.SMEM),
            pl.BlockSpec((polys, height, rows_here), lambda i: (0, jnp.minimum(i, steps - 1), 0)),
        ],
        out_specs=out_specs,
        compiler_params=pltpu.CompilerParams(vmem_limit_bytes=VMEM_BYTES),
        cost_estimate=SMALL_COST,
        name="rest_sections",
    )(table, coefficients, weights, coefficients)
    pieces = [list(outs[i * owners:(i + 1) * owners]) for i in range(len(counts))]
    return pieces, list(outs[len(counts) * owners:])


def second_kernel(group, owners, middle_ref, turn_ref, last_ref, *refs):
    piece_refs, out_ref = refs[:owners], refs[-1]
    count = out_ref.shape[2]
    share = SPLIT_HI // owners
    lines = []
    for item in range(group):
        places = pl.ds(item, 1) if share == 1 else pl.ds(item, share, stride=group)
        gathered = [
            jnp.concatenate(
                [piece_ref[poly, part, 0, places, :] for part in range(2) for piece_ref in piece_refs], axis=0
            )
            for poly in range(count)
        ]
        high, low = split(gathered[0] if count == 1 else jnp.concatenate(gathered, axis=1))
        turned = jnp.dot(
            middle_ref[item], jnp.concatenate([high, high, low], axis=0), preferred_element_type=jnp.float32
        )
        cos_turn, sin_turn = turn_ref[item, 0], turn_ref[item, 1]
        for poly in range(count):
            lanes = slice(poly * SPLIT_LO, (poly + 1) * SPLIT_LO)
            real, imag = turned[:SPLIT_HI, lanes], turned[SPLIT_HI:, lanes]
            lines.append(
                jnp.concatenate([real * cos_turn - imag * sin_turn, real * sin_turn + imag * cos_turn], axis=1)
            )
    high, low = split(jnp.concatenate(lines, axis=0))
    result = jnp.dot(jnp.concatenate([high, low, high], axis=1), last_ref[...], preferred_element_type=jnp.float32)
    for item in range(group):
        for poly in range(count):
            top = (item * count + poly) * SPLIT_HI
            out_ref[0, item, poly] = result[top:top + SPLIT_HI, :SPLIT_LO]
            out_ref[1, item, poly] = result[top:top + SPLIT_HI, SPLIT_LO:]


def second_section(tables, pieces, previous, start, count, polys, owners):
    middle, turn, last = tables
    extent = LEN_COLS // owners
    group = min(8, extent)
    together = 2 if start % 2 == 0 and count % 2 == 0 else 1
    first = start // together
    block = (together, 2, 1) + pieces[0].shape[3:]
    in_specs = [
        pl.BlockSpec((group,) + middle.shape[1:], lambda i, j: (i, 0, 0)),
        pl.BlockSpec((group,) + turn.shape[1:], lambda i, j: (i, 0, 0, 0)),
        pl.BlockSpec(last.shape, lambda i, j: (0, 0)),
    ] + [pl.BlockSpec(block, lambda i, j: (j, 0, i, 0, 0))] * owners
    operands = [middle, turn, last] + list(pieces)
    aliases = {}
    if previous is not None:
        aliases = {len(operands): 0}
        operands.append(previous)
        in_specs.append(pl.BlockSpec(memory_space=pl.ANY))
    return pl.pallas_call(
        functools.partial(second_kernel, group, owners),
        out_shape=jax.ShapeDtypeStruct((2, extent, polys, SPLIT_HI, SPLIT_LO), jnp.float32),
        grid=(extent // group, count // together),
        in_specs=in_specs,
        out_specs=pl.BlockSpec((2, group, together, SPLIT_HI, SPLIT_LO), lambda i, j: (0, i, first + j, 0, 0)),
        input_output_aliases=aliases,
        compiler_params=pltpu.CompilerParams(vmem_limit_bytes=VMEM_BYTES),
        cost_estimate=SMALL_COST,
        name="second_section",
    )(*operands)


def filter_kernel(value_ref, table_ref, carry_ref, reach_ref, out_ref):
    table_high, table_low = split(table_ref[0])
    table = jnp.concatenate([table_high, table_high, table_low], axis=0)
    reach_real, reach_imag = reach_ref[0, 0:1, :], reach_ref[0, 1:2, :]
    blocks = value_ref.shape[2] // SPLIT_LO
    for block in range(blocks):
        lanes = slice(block * SPLIT_LO, (block + 1) * SPLIT_LO)
        high, low = split(value_ref[0, :, lanes])
        local = jnp.dot(jnp.concatenate([high, low, high], axis=1), table, preferred_element_type=jnp.float32)
        real = carry_ref[0, 0, :, block:block + 1]
        imag = carry_ref[1, 0, :, block:block + 1]
        out_ref[0, 0, :, lanes] = local[:, :SPLIT_LO] + (real * reach_real - imag * reach_imag)
        out_ref[1, 0, :, lanes] = local[:, SPLIT_LO:] + (real * reach_imag + imag * reach_real)


def filter_columns(values, table, carry, reach):
    columns, extent, rows_here = values.shape
    return pl.pallas_call(
        filter_kernel,
        out_shape=jax.ShapeDtypeStruct((2,) + values.shape, jnp.float32),
        grid=(columns,),
        in_specs=[
            pl.BlockSpec((1, extent, rows_here), lambda i: (i, 0, 0)),
            pl.BlockSpec((1,) + table.shape[1:], lambda i: (i, 0, 0)),
            pl.BlockSpec((2, 1) + carry.shape[2:], lambda i: (0, i, 0, 0)),
            pl.BlockSpec((1,) + reach.shape[1:], lambda i: (i, 0, 0)),
        ],
        out_specs=pl.BlockSpec((2, 1, extent, rows_here), lambda i: (0, i, 0, 0)),
        compiler_params=pltpu.CompilerParams(vmem_limit_bytes=VMEM_BYTES),
        cost_estimate=SMALL_COST,
        name="filter_columns",
    )(values, table, carry, reach)


def times(left, right):
    return left[0] * right[0] - left[1] * right[1], left[0] * right[1] + left[1] * right[0]


def powers_of(point_index, point_cycle):
    decay = jnp.log1p((point_cycle.astype(jnp.float32) + 1.0) / 512.0)

    def powers(exponent):
        leading = (-1,) + (1,) * (exponent.ndim - 1)
        kept = jnp.exp(exponent.astype(jnp.float32) * -decay.reshape(leading))
        turns = (exponent * point_index.reshape(leading)) & (LENGTH - 1)
        angles = turns.astype(jnp.float32) * (2.0 * math.pi / LENGTH)
        return kept * jnp.cos(angles), kept * jnp.sin(angles)

    return powers


def masked(keep, pair):
    return jnp.where(keep, pair[0], 0.0), jnp.where(keep, pair[1], 0.0)


def segment_states(values, point_index, point_cycle):
    columns, extent, rows_here = values.shape
    blocks = rows_here // SPLIT_LO
    powers = powers_of(point_index, point_cycle)
    offset = jnp.arange(rows_here, dtype=jnp.int32)[None, :, None]
    border = SPLIT_LO * (1 + jnp.arange(blocks, dtype=jnp.int32))[None, None, :]
    distance = border - 1 - offset
    weights = masked(distance >= 0, powers(jnp.maximum(distance, 0)))
    weights = jnp.concatenate(weights, axis=2)
    ends = jnp.einsum("jnm,jmq->jnq", values, weights, precision=precise)
    return ends.reshape(columns, extent, 2, blocks).transpose(2, 0, 1, 3)


def from_all_owners(ends):
    owners = LEN_ROWS // (ends.shape[3] * SPLIT_LO)
    last = ends[:, :, :, -1]
    if owners <= 8:
        moved = [lax.ppermute(last, "coef", [(i, (i + far) % owners) for i in range(owners)]) for far in range(1, owners)]
        return jnp.stack([last] + moved)
    gathered = lax.all_gather(last, "coef", axis=0)
    return gathered[(lax.axis_index("coef") - jnp.arange(owners)) % owners]


def quotient_columns(values, ends, gathered, offsets, point_index, point_cycle):
    columns, extent, rows_here = values.shape
    blocks = rows_here // SPLIT_LO
    owners = LEN_ROWS // rows_here
    here = lax.axis_index("coef")
    powers = powers_of(point_index, point_cycle)

    owner = (here - jnp.arange(owners, dtype=jnp.int32)) % owners
    weigh = powers(rows_here * (owners - 1 - owner)[None, :, None])
    segment = (gathered[:, 0].transpose(1, 0, 2), gathered[:, 1].transpose(1, 0, 2))
    row_end = times(weigh, segment)
    row_end = (jnp.sum(row_end[0], axis=1), jnp.sum(row_end[1], axis=1))
    radius = 1.0 + (point_cycle.astype(jnp.float32) + 1.0) / 512.0
    angle = point_index.astype(jnp.float32) * (2.0 * math.pi / LENGTH)
    point = (radius * jnp.cos(angle), -radius * jnp.sin(angle))
    shift = times(point, (offsets[0] * math.sqrt(LENGTH), offsets[1] * math.sqrt(LENGTH)))
    final = jnp.arange(extent, dtype=jnp.int32)[None, :] == extent - 1
    row_end = tuple(value - jnp.where(final, moved[:, None], 0.0) for value, moved in zip(row_end, shift))
    row = jnp.arange(extent, dtype=jnp.int32)
    since = (row[:, None] - row[None, :] - 1) % extent
    kernel = powers(LEN_ROWS * since[None])
    around = 1.0 / (1.0 - jnp.exp(-float(LENGTH) * jnp.log1p((point_cycle.astype(jnp.float32) + 1.0) / 512.0)))
    kernel = (kernel[0] * around[:, None, None], kernel[1] * around[:, None, None])

    def apply(matrix, vector):
        return jnp.sum(matrix * vector[:, None, :], axis=2)

    row_start = (
        apply(kernel[0], row_end[0]) - apply(kernel[1], row_end[1]),
        apply(kernel[0], row_end[1]) + apply(kernel[1], row_end[0]),
    )

    ahead = here - 1 - owner
    within = times(masked(ahead >= 0, powers(rows_here * jnp.maximum(ahead, 0)[None, :])), (1.0, 0.0))
    within = times((within[0][:, :, None], within[1][:, :, None]), segment)
    segment_start = times(powers((rows_here * here)[None, None]), row_start)
    segment_start = tuple(start + jnp.sum(part, axis=1) for start, part in zip(segment_start, within))
    block = SPLIT_LO * jnp.arange(blocks, dtype=jnp.int32)[None, None, :]
    carry = times(powers(block), (segment_start[0][:, :, None], segment_start[1][:, :, None]))
    carry = jnp.stack(carry) + jnp.pad(ends[:, :, :, : blocks - 1], ((0, 0), (0, 0), (0, 0), (1, 0)))

    lane = jnp.arange(SPLIT_LO, dtype=jnp.int32)
    apart = (lane[None, :] - lane[:, None])[None]
    inside = masked(apart >= 0, powers(jnp.maximum(apart, 0) + 1))
    table = -jnp.concatenate(inside, axis=2)
    reach = -jnp.stack(powers((lane + 2)[None, :]), axis=1)
    return filter_columns(values, table, carry, reach)


def chunk_sizes(polys):
    return [4, 5, 2, 1] if polys==12 else [1,2,2,1]


def exchange(pieces, owners, sent):
    if owners <= 8:
        moved = [pieces[0]]
        for far in range(1, owners):
            piece = pieces[far]
            if len(sent) >= DEPTH:
                chunk, place = sent[-DEPTH]
                piece, chunk[place] = lax.optimization_barrier((piece, chunk[place]))
            moved.append(lax.ppermute(piece, "coef", [(i, (i + far) % owners) for i in range(owners)]))
            sent.append((moved, far))
        return moved
    here = lax.axis_index("coef")
    stacked = jnp.roll(jnp.stack(pieces), here, axis=0)
    stacked = lax.all_to_all(stacked, "coef", split_axis=0, concat_axis=0, tiled=True)
    stacked = jnp.roll(stacked[::-1], here + 1, axis=0)
    return [stacked[far] for far in range(owners)]


def shift_sum(pieces, axis):
    size = len(pieces)
    total = pieces[0]
    for far in range(1, size):
        total = total + lax.ppermute(pieces[far], axis, [(i, (i + far) % size) for i in range(size)])
    return total


def shards(coefficients, batch_weights, claimed, point_index, point_cycle, sizes):
    owners, poly_size, limb_size = sizes
    polys = coefficients.shape[0]
    extent = LEN_COLS // owners
    table = jnp.asarray(first_table(owners))
    begin = lax.axis_index("coef") * extent
    tables = (
        lax.dynamic_slice_in_dim(jnp.asarray(middle_table(owners)), begin, extent, axis=0),
        lax.dynamic_slice_in_dim(jnp.asarray(turn_table()), begin, extent, axis=0),
        jnp.asarray(last_table()),
    )

    chunks = []
    start = 0
    for count in chunk_sizes(polys):
        chunks.append((start, count))
        start += count

    columns = batch_weights.shape[0] // (poly_size * limb_size)
    me_poly, me_limb = lax.axis_index("poly"), lax.axis_index("limb")
    ahead = (me_poly + jnp.arange(poly_size, dtype=jnp.int32)[None, :]) % poly_size
    aside = (me_limb + jnp.arange(limb_size, dtype=jnp.int32)[:, None]) % limb_size
    target = (ahead * limb_size + aside).reshape(-1)
    weights = batch_weights.reshape(-1, columns, polys)[target].reshape(batch_weights.shape)

    counts = [count for _, count in chunks]
    made = [first_section(table, coefficients, counts[0], owners)]
    others, batched = rest_sections(table, coefficients, counts[0], counts[1:], owners, weights, limb_size)
    made += others
    offsets = jnp.sum(batch_weights[None] * claimed, axis=2)

    arrived = []
    sent = []
    used = 0
    evaluations = None
    for number, pieces in enumerate(made):
        if number >= 2:
            evaluations = second_section(tables, arrived[used], evaluations, *chunks[used], polys, owners)
            used += 1
            tied = None
            if number == 2:
                tied = segment_states(values, point_index, point_cycle)
            elif number == 3:
                gathered = from_all_owners(ends)
                tied = quotient_columns(values, ends, gathered, offsets, point_index, point_cycle)
            pieces, tied, evaluations = lax.optimization_barrier((pieces, tied, evaluations))
            if number == 2:
                ends = tied
            elif number == 3:
                quotient = tied
        arrived.append(exchange(pieces, owners, sent))
        if number == 0:
            batched, arrived[0][2:] = lax.optimization_barrier((batched, arrived[0][2:]))
            moved = [batched[0]] + [
                lax.ppermute(batched[far], "limb", [(i, (i + far) % limb_size) for i in range(limb_size)])
                for far in range(1, limb_size)
            ]
        if number == 1:
            sums = functools.reduce(jnp.add, moved)
            values = shift_sum([sums[i * columns:(i + 1) * columns] for i in range(poly_size)], "poly")
            offsets = shift_sum([shift_sum([offsets] * limb_size, "limb")] * poly_size, "poly")
            offsets = lax.dynamic_slice_in_dim(offsets, (me_poly * limb_size + me_limb) * columns, columns, axis=1)

    for number in range(used, len(chunks)):
        evaluations = second_section(tables, arrived[number], evaluations, *chunks[number], polys, owners)
    return (evaluations, quotient)


def solution(mesh):
    placed = (
        P(("parts", "poly", "limb"), None, "coef"),
        P("parts", ("poly", "limb")),
        P(None, "parts", ("poly", "limb")),
        P(("parts", "poly", "limb")),
        P(("parts", "poly", "limb")),
    )
    return jax.shard_map(
        functools.partial(shards, sizes=tuple(mesh.shape[name] for name in ("coef", "poly", "limb"))),
        mesh=mesh,
        in_specs=placed,
        out_specs=(
            P(None, "coef", ("parts", "poly", "limb"), None, None),
            P(None, ("parts", "poly", "limb"), None, "coef"),
        ),
        check_vma=False,
    )
```

```python
import functools
import math

import jax
import jax.numpy as jnp
import ml_dtypes
import numpy as np
from jax import lax
from jax.experimental import pallas as pl
from jax.experimental.pallas import tpu as pltpu
from jax.sharding import PartitionSpec as P

LEN_COLS = 128
SPLIT_HI = 32
SPLIT_LO = 128
LEN_ROWS = 4096
LENGTH = 524288
VMEM_BYTES = 48 * 2**20

SMALL_COST = pl.CostEstimate(flops=1, bytes_accessed=1, transcendentals=0)
DEPTH = 5

precise = lax.Precision.HIGHEST


def split(value):
    high = value.astype(jnp.bfloat16)
    low = (value - high.astype(jnp.float32)).astype(jnp.bfloat16)
    return high, low


def split_host(value):
    value = np.asarray(value, np.float32)
    high = value.astype(ml_dtypes.bfloat16)
    low = (value - high.astype(np.float32)).astype(ml_dtypes.bfloat16)
    return high, low


def roots(exponent, length):
    angles = np.asarray(exponent % length, np.float64) * (-2.0 * math.pi / length)
    return np.cos(angles), np.sin(angles)


def first_table(owners):
    index = np.arange(LEN_COLS, dtype=np.int64)
    pair = np.stack(roots(index[:, None] * index[None, :], LEN_COLS)) / math.sqrt(LEN_COLS)
    extent = LEN_COLS // owners
    table = pair.reshape(2, owners, extent, LEN_COLS).transpose(1, 0, 2, 3)
    table = table.reshape(2 * LEN_COLS, LEN_COLS)
    return np.concatenate([table, table]).astype(np.float32)


def middle_table(owners):
    frequency = np.arange(LEN_COLS, dtype=np.int64)
    extent = LEN_COLS // owners
    share = SPLIT_HI // owners
    sender = (frequency[:, None] // extent - np.arange(owners)[None, :]) % owners
    place = (sender[:, :, None] * share + np.arange(share)).reshape(LEN_COLS, 1, SPLIT_HI)
    slow = np.arange(SPLIT_HI, dtype=np.int64)[None, :, None]
    real, imag = roots(place * (LEN_COLS * slow + frequency[:, None, None]), LEN_ROWS)
    table = np.concatenate(
        [np.concatenate([real, -imag], axis=2), np.concatenate([imag, real], axis=2)], axis=1
    )
    high, low = split_host(table / math.sqrt(SPLIT_HI))
    return np.concatenate([high, low, high], axis=2)


def turn_table():
    frequency = np.arange(LEN_COLS, dtype=np.int64)[:, None, None]
    slow = np.arange(SPLIT_HI, dtype=np.int64)[None, :, None]
    fast = np.arange(SPLIT_LO, dtype=np.int64)[None, None, :]
    return np.stack(roots(fast * (frequency + LEN_COLS * slow), LENGTH), axis=1).astype(np.float32)


def last_table():
    index = np.arange(SPLIT_LO, dtype=np.int64)
    real, imag = roots(index[:, None] * index[None, :], SPLIT_LO)
    table = np.concatenate(
        [np.concatenate([real, imag], axis=1), np.concatenate([-imag, real], axis=1)], axis=0
    )
    high, low = split_host(table / math.sqrt(SPLIT_LO))
    return np.concatenate([high, high, low], axis=0)


def transform(group, table_ref, coeff_ref, out_refs):
    owners = len(out_refs)
    rows = table_ref.shape[0] // 2
    each = rows // owners
    extent = each // 2
    begin = pl.multiple_of(lax.axis_index("coef") * each, each)
    high, low = split(table_ref[pl.ds(begin, rows), :])
    left = jnp.concatenate([high, low, high], axis=1)
    blocks = coeff_ref.shape[2] // SPLIT_LO
    step = min(2, blocks)
    for lane in range(0, blocks, step):
        value_high, value_low = split(coeff_ref[0, :, lane * SPLIT_LO:(lane + step) * SPLIT_LO])
        right = jnp.concatenate([value_high, value_high, value_low], axis=0)
        result = jnp.dot(left, right, preferred_element_type=jnp.float32)
        for inner in range(step):
            for owner in range(owners):
                for part in range(2):
                    for batch in range(extent // group):
                        top = owner * each + part * extent + batch * group
                        out_refs[owner][0, part, batch, pl.ds((lane + inner) * group, group), :] = result[
                            top:top + group, inner * SPLIT_LO:(inner + 1) * SPLIT_LO
                        ]


def batch(weight_ref, coeff_ref, out_refs):
    polys = coeff_ref.shape[0]
    lanes = min(512, coeff_ref.shape[2])
    for top in range(0, coeff_ref.shape[1], 8):
        for lane in range(0, coeff_ref.shape[2], lanes):
            here = (slice(top, top + 8), slice(lane, lane + lanes))
            for target, out_ref in enumerate(out_refs):
                for column in range(out_ref.shape[0]):
                    row = target * out_ref.shape[0] + column
                    total = weight_ref[row, 0] * coeff_ref[(0,) + here]
                    for poly in range(1, polys):
                        total = total + weight_ref[row, poly] * coeff_ref[(poly,) + here]
                    out_ref[(column,) + here] = total


def first_kernel(group, table_ref, coeff_ref, *out_refs):
    transform(group, table_ref, coeff_ref, out_refs)


def rest_kernel(group, counts, owners, table_ref, coeff_ref, weight_ref, rows_ref, *out_refs):
    step = pl.program_id(0)
    batch(weight_ref, rows_ref, out_refs[owners * len(counts):])
    begin = 0
    for number, count in enumerate(counts):

        @pl.when((step >= begin) & (step < begin + count))
        def _(number=number):
            transform(group, table_ref, coeff_ref, out_refs[number * owners:(number + 1) * owners])

        begin += count


def piece_shape(coefficients, count, owners):
    extent = LEN_COLS // owners
    group = min(8, extent)
    return (count, 2, extent // group, (coefficients.shape[2] // SPLIT_LO) * group, SPLIT_LO)


def first_section(table, coefficients, count, owners):
    rows_here = coefficients.shape[2]
    shape = piece_shape(coefficients, count, owners)
    pieces = pl.pallas_call(
        functools.partial(first_kernel, min(8, LEN_COLS // owners)),
        out_shape=[jax.ShapeDtypeStruct(shape, jnp.float32)] * owners,
        grid=(count,),
        in_specs=[
            pl.BlockSpec(table.shape, lambda i: (0, 0)),
            pl.BlockSpec((1, LEN_COLS, rows_here), lambda i: (i, 0, 0)),
        ],
        out_specs=[pl.BlockSpec((1,) + shape[1:], lambda i: (i, 0, 0, 0, 0))] * owners,
        compiler_params=pltpu.CompilerParams(vmem_limit_bytes=VMEM_BYTES),
        cost_estimate=SMALL_COST,
        name="first_section",
    )(table, coefficients)
    return list(pieces)


def rest_sections(table, coefficients, start, counts, owners, weights, targets):
    polys, _, rows_here = coefficients.shape
    columns = weights.shape[0] // targets
    total = sum(counts)
    height = 8
    steps = LEN_COLS // height
    out_specs, out_shape = [], []
    begin = 0
    for count in counts:
        shape = piece_shape(coefficients, count, owners)
        place = lambda i, begin=begin, count=count: (jnp.clip(i - begin, 0, count - 1), 0, 0, 0, 0)
        out_specs += [pl.BlockSpec((1,) + shape[1:], place)] * owners
        out_shape += [jax.ShapeDtypeStruct(shape, jnp.float32)] * owners
        begin += count
    out_specs += [pl.BlockSpec((columns, height, rows_here), lambda i: (0, jnp.minimum(i, steps - 1), 0))] * targets
    out_shape += [jax.ShapeDtypeStruct((columns, LEN_COLS, rows_here), jnp.float32)] * targets
    outs = pl.pallas_call(
        functools.partial(rest_kernel, min(8, LEN_COLS // owners), tuple(counts), owners),
        out_shape=out_shape,
        grid=(max(steps, total),),
        in_specs=[
            pl.BlockSpec(table.shape, lambda i: (0, 0)),
            pl.BlockSpec((1, LEN_COLS, rows_here), lambda i: (start + jnp.minimum(i, total - 1), 0, 0)),
            pl.BlockSpec(memory_space=pltpu.SMEM),
            pl.BlockSpec((polys, height, rows_here), lambda i: (0, jnp.minimum(i, steps - 1), 0)),
        ],
        out_specs=out_specs,
        compiler_params=pltpu.CompilerParams(vmem_limit_bytes=VMEM_BYTES),
        cost_estimate=SMALL_COST,
        name="rest_sections",
    )(table, coefficients, weights, coefficients)
    pieces = [list(outs[i * owners:(i + 1) * owners]) for i in range(len(counts))]
    return pieces, list(outs[len(counts) * owners:])


def second_kernel(group, owners, middle_ref, turn_ref, last_ref, *refs):
    piece_refs, out_ref = refs[:owners], refs[-1]
    count = out_ref.shape[2]
    share = SPLIT_HI // owners
    lines = []
    for item in range(group):
        places = pl.ds(item, 1) if share == 1 else pl.ds(item, share, stride=group)
        gathered = [
            jnp.concatenate(
                [piece_ref[poly, part, 0, places, :] for part in range(2) for piece_ref in piece_refs], axis=0
            )
            for poly in range(count)
        ]
        high, low = split(gathered[0] if count == 1 else jnp.concatenate(gathered, axis=1))
        turned = jnp.dot(
            middle_ref[item], jnp.concatenate([high, high, low], axis=0), preferred_element_type=jnp.float32
        )
        cos_turn, sin_turn = turn_ref[item, 0], turn_ref[item, 1]
        for poly in range(count):
            lanes = slice(poly * SPLIT_LO, (poly + 1) * SPLIT_LO)
            real, imag = turned[:SPLIT_HI, lanes], turned[SPLIT_HI:, lanes]
            lines.append(
                jnp.concatenate([real * cos_turn - imag * sin_turn, real * sin_turn + imag * cos_turn], axis=1)
            )
    high, low = split(jnp.concatenate(lines, axis=0))
    result = jnp.dot(jnp.concatenate([high, low, high], axis=1), last_ref[...], preferred_element_type=jnp.float32)
    for item in range(group):
        for poly in range(count):
            top = (item * count + poly) * SPLIT_HI
            out_ref[0, item, poly] = result[top:top + SPLIT_HI, :SPLIT_LO]
            out_ref[1, item, poly] = result[top:top + SPLIT_HI, SPLIT_LO:]


def second_section(tables, pieces, previous, start, count, polys, owners):
    middle, turn, last = tables
    extent = LEN_COLS // owners
    group = min(8, extent)
    together = 2 if start % 2 == 0 and count % 2 == 0 else 1
    first = start // together
    block = (together, 2, 1) + pieces[0].shape[3:]
    in_specs = [
        pl.BlockSpec((group,) + middle.shape[1:], lambda i, j: (i, 0, 0)),
        pl.BlockSpec((group,) + turn.shape[1:], lambda i, j: (i, 0, 0, 0)),
        pl.BlockSpec(last.shape, lambda i, j: (0, 0)),
    ] + [pl.BlockSpec(block, lambda i, j: (j, 0, i, 0, 0))] * owners
    operands = [middle, turn, last] + list(pieces)
    aliases = {}
    if previous is not None:
        aliases = {len(operands): 0}
        operands.append(previous)
        in_specs.append(pl.BlockSpec(memory_space=pl.ANY))
    return pl.pallas_call(
        functools.partial(second_kernel, group, owners),
        out_shape=jax.ShapeDtypeStruct((2, extent, polys, SPLIT_HI, SPLIT_LO), jnp.float32),
        grid=(extent // group, count // together),
        in_specs=in_specs,
        out_specs=pl.BlockSpec((2, group, together, SPLIT_HI, SPLIT_LO), lambda i, j: (0, i, first + j, 0, 0)),
        input_output_aliases=aliases,
        compiler_params=pltpu.CompilerParams(vmem_limit_bytes=VMEM_BYTES),
        cost_estimate=SMALL_COST,
        name="second_section",
    )(*operands)


def filter_kernel(value_ref, table_ref, carry_ref, reach_ref, out_ref):
    table_high, table_low = split(table_ref[0])
    table = jnp.concatenate([table_high, table_high, table_low], axis=0)
    reach_real, reach_imag = reach_ref[0, 0:1, :], reach_ref[0, 1:2, :]
    blocks = value_ref.shape[2] // SPLIT_LO
    for block in range(blocks):
        lanes = slice(block * SPLIT_LO, (block + 1) * SPLIT_LO)
        high, low = split(value_ref[0, :, lanes])
        local = jnp.dot(jnp.concatenate([high, low, high], axis=1), table, preferred_element_type=jnp.float32)
        real = carry_ref[0, 0, :, block:block + 1]
        imag = carry_ref[1, 0, :, block:block + 1]
        out_ref[0, 0, :, lanes] = local[:, :SPLIT_LO] + (real * reach_real - imag * reach_imag)
        out_ref[1, 0, :, lanes] = local[:, SPLIT_LO:] + (real * reach_imag + imag * reach_real)


def filter_columns(values, table, carry, reach):
    columns, extent, rows_here = values.shape
    return pl.pallas_call(
        filter_kernel,
        out_shape=jax.ShapeDtypeStruct((2,) + values.shape, jnp.float32),
        grid=(columns,),
        in_specs=[
            pl.BlockSpec((1, extent, rows_here), lambda i: (i, 0, 0)),
            pl.BlockSpec((1,) + table.shape[1:], lambda i: (i, 0, 0)),
            pl.BlockSpec((2, 1) + carry.shape[2:], lambda i: (0, i, 0, 0)),
            pl.BlockSpec((1,) + reach.shape[1:], lambda i: (i, 0, 0)),
        ],
        out_specs=pl.BlockSpec((2, 1, extent, rows_here), lambda i: (0, i, 0, 0)),
        compiler_params=pltpu.CompilerParams(vmem_limit_bytes=VMEM_BYTES),
        cost_estimate=SMALL_COST,
        name="filter_columns",
    )(values, table, carry, reach)


def times(left, right):
    return left[0] * right[0] - left[1] * right[1], left[0] * right[1] + left[1] * right[0]


def powers_of(point_index, point_cycle):
    decay = jnp.log1p((point_cycle.astype(jnp.float32) + 1.0) / 512.0)

    def powers(exponent):
        leading = (-1,) + (1,) * (exponent.ndim - 1)
        kept = jnp.exp(exponent.astype(jnp.float32) * -decay.reshape(leading))
        turns = (exponent * point_index.reshape(leading)) & (LENGTH - 1)
        angles = turns.astype(jnp.float32) * (2.0 * math.pi / LENGTH)
        return kept * jnp.cos(angles), kept * jnp.sin(angles)

    return powers


def masked(keep, pair):
    return jnp.where(keep, pair[0], 0.0), jnp.where(keep, pair[1], 0.0)


def segment_states(values, point_index, point_cycle):
    columns, extent, rows_here = values.shape
    blocks = rows_here // SPLIT_LO
    powers = powers_of(point_index, point_cycle)
    offset = jnp.arange(rows_here, dtype=jnp.int32)[None, :, None]
    border = SPLIT_LO * (1 + jnp.arange(blocks, dtype=jnp.int32))[None, None, :]
    distance = border - 1 - offset
    weights = masked(distance >= 0, powers(jnp.maximum(distance, 0)))
    weights = jnp.concatenate(weights, axis=2)
    ends = jnp.einsum("jnm,jmq->jnq", values, weights, precision=precise)
    return ends.reshape(columns, extent, 2, blocks).transpose(2, 0, 1, 3)


def from_all_owners(ends):
    owners = LEN_ROWS // (ends.shape[3] * SPLIT_LO)
    last = ends[:, :, :, -1]
    if owners <= 8:
        moved = [lax.ppermute(last, "coef", [(i, (i + far) % owners) for i in range(owners)]) for far in range(1, owners)]
        return jnp.stack([last] + moved)
    gathered = lax.all_gather(last, "coef", axis=0)
    return gathered[(lax.axis_index("coef") - jnp.arange(owners)) % owners]


def quotient_columns(values, ends, gathered, offsets, point_index, point_cycle):
    columns, extent, rows_here = values.shape
    blocks = rows_here // SPLIT_LO
    owners = LEN_ROWS // rows_here
    here = lax.axis_index("coef")
    powers = powers_of(point_index, point_cycle)

    owner = (here - jnp.arange(owners, dtype=jnp.int32)) % owners
    weigh = powers(rows_here * (owners - 1 - owner)[None, :, None])
    segment = (gathered[:, 0].transpose(1, 0, 2), gathered[:, 1].transpose(1, 0, 2))
    row_end = times(weigh, segment)
    row_end = (jnp.sum(row_end[0], axis=1), jnp.sum(row_end[1], axis=1))
    radius = 1.0 + (point_cycle.astype(jnp.float32) + 1.0) / 512.0
    angle = point_index.astype(jnp.float32) * (2.0 * math.pi / LENGTH)
    point = (radius * jnp.cos(angle), -radius * jnp.sin(angle))
    shift = times(point, (offsets[0] * math.sqrt(LENGTH), offsets[1] * math.sqrt(LENGTH)))
    final = jnp.arange(extent, dtype=jnp.int32)[None, :] == extent - 1
    row_end = tuple(value - jnp.where(final, moved[:, None], 0.0) for value, moved in zip(row_end, shift))
    row = jnp.arange(extent, dtype=jnp.int32)
    since = (row[:, None] - row[None, :] - 1) % extent
    kernel = powers(LEN_ROWS * since[None])
    around = 1.0 / (1.0 - jnp.exp(-float(LENGTH) * jnp.log1p((point_cycle.astype(jnp.float32) + 1.0) / 512.0)))
    kernel = (kernel[0] * around[:, None, None], kernel[1] * around[:, None, None])

    def apply(matrix, vector):
        return jnp.sum(matrix * vector[:, None, :], axis=2)

    row_start = (
        apply(kernel[0], row_end[0]) - apply(kernel[1], row_end[1]),
        apply(kernel[0], row_end[1]) + apply(kernel[1], row_end[0]),
    )

    ahead = here - 1 - owner
    within = times(masked(ahead >= 0, powers(rows_here * jnp.maximum(ahead, 0)[None, :])), (1.0, 0.0))
    within = times((within[0][:, :, None], within[1][:, :, None]), segment)
    segment_start = times(powers((rows_here * here)[None, None]), row_start)
    segment_start = tuple(start + jnp.sum(part, axis=1) for start, part in zip(segment_start, within))
    block = SPLIT_LO * jnp.arange(blocks, dtype=jnp.int32)[None, None, :]
    carry = times(powers(block), (segment_start[0][:, :, None], segment_start[1][:, :, None]))
    carry = jnp.stack(carry) + jnp.pad(ends[:, :, :, : blocks - 1], ((0, 0), (0, 0), (0, 0), (1, 0)))

    lane = jnp.arange(SPLIT_LO, dtype=jnp.int32)
    apart = (lane[None, :] - lane[:, None])[None]
    inside = masked(apart >= 0, powers(jnp.maximum(apart, 0) + 1))
    table = -jnp.concatenate(inside, axis=2)
    reach = -jnp.stack(powers((lane + 2)[None, :]), axis=1)
    return filter_columns(values, table, carry, reach)


def chunk_sizes(polys):
    first, third = max(1, polys // 3), max(1, polys // 6)
    return [first, polys - first - third - 1, third, 1]


def exchange(pieces, owners, sent):
    if owners <= 8:
        moved = [pieces[0]]
        for far in range(1, owners):
            piece = pieces[far]
            if len(sent) >= DEPTH:
                chunk, place = sent[-DEPTH]
                piece, chunk[place] = lax.optimization_barrier((piece, chunk[place]))
            moved.append(lax.ppermute(piece, "coef", [(i, (i + far) % owners) for i in range(owners)]))
            sent.append((moved, far))
        return moved
    here = lax.axis_index("coef")
    stacked = jnp.roll(jnp.stack(pieces), here, axis=0)
    stacked = lax.all_to_all(stacked, "coef", split_axis=0, concat_axis=0, tiled=True)
    stacked = jnp.roll(stacked[::-1], here + 1, axis=0)
    return [stacked[far] for far in range(owners)]


def shift_sum(pieces, axis):
    size = len(pieces)
    total = pieces[0]
    for far in range(1, size):
        total = total + lax.ppermute(pieces[far], axis, [(i, (i + far) % size) for i in range(size)])
    return total


def shards(coefficients, batch_weights, claimed, point_index, point_cycle, sizes):
    owners, poly_size, limb_size = sizes
    polys = coefficients.shape[0]
    extent = LEN_COLS // owners
    table = jnp.asarray(first_table(owners))
    begin = lax.axis_index("coef") * extent
    tables = (
        lax.dynamic_slice_in_dim(jnp.asarray(middle_table(owners)), begin, extent, axis=0),
        lax.dynamic_slice_in_dim(jnp.asarray(turn_table()), begin, extent, axis=0),
        jnp.asarray(last_table()),
    )

    chunks = []
    start = 0
    for count in chunk_sizes(polys):
        chunks.append((start, count))
        start += count

    columns = batch_weights.shape[0] // (poly_size * limb_size)
    me_poly, me_limb = lax.axis_index("poly"), lax.axis_index("limb")
    ahead = (me_poly + jnp.arange(poly_size, dtype=jnp.int32)[None, :]) % poly_size
    aside = (me_limb + jnp.arange(limb_size, dtype=jnp.int32)[:, None]) % limb_size
    target = (ahead * limb_size + aside).reshape(-1)
    weights = batch_weights.reshape(-1, columns, polys)[target].reshape(batch_weights.shape)

    counts = [count for _, count in chunks]
    made = [first_section(table, coefficients, counts[0], owners)]
    others, batched = rest_sections(table, coefficients, counts[0], counts[1:], owners, weights, limb_size)
    made += others
    offsets = jnp.sum(batch_weights[None] * claimed, axis=2)

    arrived = []
    sent = []
    used = 0
    evaluations = None
    for number, pieces in enumerate(made):
        if number >= 2:
            evaluations = second_section(tables, arrived[used], evaluations, *chunks[used], polys, owners)
            used += 1
            tied = None
            if number == 2:
                tied = segment_states(values, point_index, point_cycle)
            elif number == 3:
                gathered = from_all_owners(ends)
                tied = quotient_columns(values, ends, gathered, offsets, point_index, point_cycle)
            pieces, tied, evaluations = lax.optimization_barrier((pieces, tied, evaluations))
            if number == 2:
                ends = tied
            elif number == 3:
                quotient = tied
        arrived.append(exchange(pieces, owners, sent))
        if number == 0:
            batched, arrived[0][2:] = lax.optimization_barrier((batched, arrived[0][2:]))
            moved = [batched[0]] + [
                lax.ppermute(batched[far], "limb", [(i, (i + far) % limb_size) for i in range(limb_size)])
                for far in range(1, limb_size)
            ]
        if number == 1:
            sums = functools.reduce(jnp.add, moved)
            values = shift_sum([sums[i * columns:(i + 1) * columns] for i in range(poly_size)], "poly")
            offsets = shift_sum([shift_sum([offsets] * limb_size, "limb")] * poly_size, "poly")
            offsets = lax.dynamic_slice_in_dim(offsets, (me_poly * limb_size + me_limb) * columns, columns, axis=1)

    for number in range(used, len(chunks)):
        evaluations = second_section(tables, arrived[number], evaluations, *chunks[number], polys, owners)
    return (evaluations, quotient)


def solution(mesh):
    placed = (
        P(("parts", "poly", "limb"), None, "coef"),
        P("parts", ("poly", "limb")),
        P(None, "parts", ("poly", "limb")),
        P(("parts", "poly", "limb")),
        P(("parts", "poly", "limb")),
    )
    return jax.shard_map(
        functools.partial(shards, sizes=tuple(mesh.shape[name] for name in ("coef", "poly", "limb"))),
        mesh=mesh,
        in_specs=placed,
        out_specs=(
            P(None, "coef", ("parts", "poly", "limb"), None, None),
            P(None, ("parts", "poly", "limb"), None, "coef"),
        ),
        check_vma=False,
    )
```
